32 devices in a mesh: grp: 4 (over y, core), tile: 8 (over z, x).
Axes of the slice: x: 2, y: 2, z: 4, core: 2. Of those that a mesh axis runs over, the one named last changes fastest.
Arguments:
- adjoint_state: float32 [64, 128, 2048], P('tile', 'grp'), may hold values from -6 to 6
- misfit: float32 [64, 128, 2048], P('tile', 'grp'), may hold values from -4 to 4
- east_speed: float32 [64, 128, 2048], P('tile', 'grp'), may hold values from -0.6 to 0.6
- north_speed: float32 [64, 128, 2048], P('tile', 'grp'), may hold values from -0.6 to 0.6
- land_mask: int32 [64, 128, 2048], P('tile', 'grp'), may hold values 0 or 1
- warming_forcing_selector: int32 [128, 2048], P('grp', 'tile'), may hold values 0 or 1
- vertical_filter_matrix: float32 [64, 64], replicated, may hold values from 0 to 0.54
Outputs:
- filtered_thermal_sensitivity: float32 [64, 128, 2048], P('tile', 'grp')
- boundary_warming_sensitivity: float32 [128, 2048], P('grp', 'tile')
The draws below stay inside these ranges and needn't reach their ends.
All inputs are finite; a program needn't handle non-finite values. No bound on the sum of `land_mask` or of `warming_forcing_selector` on one device may be relied on, other than what follows from the above.
Results may differ from the reference program's by a relative error of at most 0.000088.
Values sent between devices are 32-bit elements; how exact they have to be, the bound alone decides.
A program may use at most 192 MiB of HBM per device.

```python
import jax
import jax.numpy as jnp
from jax import lax

LEV = 64
STEPS = 2
NY = 128
NX = 2048


def draw_vertical_filter_matrix(key, part):
    depth_level_index = jnp.arange(LEV)
    spacing_between = jnp.abs(depth_level_index[:, None] - depth_level_index[None, :]).astype(jnp.float32)
    factor = jax.random.uniform(key, (LEV, LEV), jnp.float32, 0.5, 1.5)
    return 0.3 * jnp.exp(-spacing_between / 3.0) * factor


def with_ends(result, key, least, high):
    spot = [jax.random.randint(jax.random.fold_in(key, axis), (), 0, length) for axis, length in enumerate(result.shape)]
    widest = result.shape.index(max(result.shape))
    beside = spot[:widest] + [(spot[widest] + 1) % result.shape[widest]] + spot[widest + 1:]
    return result.at[tuple(spot)].set(least).at[tuple(beside)].set(high)


def steps_of(key, shape, shards, least, high):
    level, own = 1.0, jax.random.fold_in(key, 6)
    for dim, parts in shards:
        draws = jnp.exp(jax.random.uniform(jax.random.fold_in(own, dim), (parts,), jnp.float32, least / len(shards), high / len(shards)))
        level = level * jnp.repeat(draws, shape[dim] // parts).reshape([-1 if axis == dim else 1 for axis in range(len(shape))])
    return level


def centred(key, extent, deviation, reach, split=(), held_as=jnp.bfloat16):
    values = deviation * jax.random.normal(key, extent, jnp.float32)
    if split:
        values = values * steps_of(key, extent, split, -0.22, 0.18)
    return jnp.clip(values, -reach, reach).astype(held_as)


def setup_inputs(seed: int = 0) -> dict:
    key_of = jax.random.split(jax.random.key(seed), 8)
    adjoint_state = centred(key_of[0], (LEV, NY, NX), 1.0, 6.0, ((0, 8), (1, 4)), jnp.float32)
    misfit = centred(key_of[1], (LEV, NY, NX), 0.5, 4.0, ((0, 8), (1, 4)), jnp.float32)
    east_speed = jnp.clip(jax.random.uniform(key_of[2], (LEV, NY, NX), jnp.float32, -0.6, 0.6) * steps_of(key_of[2], (LEV, NY, NX), ((0, 8), (1, 4)), -0.4, 0.0), -0.6, 0.6)
    north_speed = jnp.clip(jax.random.uniform(key_of[3], (LEV, NY, NX), jnp.float32, -0.6, 0.6) * steps_of(key_of[3], (LEV, NY, NX), ((0, 8), (1, 4)), -0.4, 0.0), -0.6, 0.6)
    land_mask = with_ends((jax.random.randint(key_of[4], (LEV, NY, NX), 0, 6) < 5).astype(jnp.int32), jax.random.fold_in(key_of[4], 1), 0, 1)
    warming_forcing_selector = with_ends((jax.random.randint(key_of[5], (NY, NX), 0, 3) < 1).astype(jnp.int32), jax.random.fold_in(key_of[5], 1), 0, 1)
    vertical_filter_matrix = draw_vertical_filter_matrix(jax.random.fold_in(key_of[7], 71), 0)
    return {"adjoint_state": adjoint_state, "misfit": misfit, "east_speed": east_speed, "north_speed": north_speed, "land_mask": land_mask, "warming_forcing_selector": warming_forcing_selector, "vertical_filter_matrix": vertical_filter_matrix}


def advance(padded, misfit, east_speed, north_speed, wet_cells):
    center = padded[1:-1, 1:-1, 1:-1]
    east_cell = padded[1:-1, 1:-1, 2:]
    western_neighbour = padded[1:-1, 1:-1, :-2]
    north_cell = padded[1:-1, 2:, 1:-1]
    south_cell = padded[1:-1, :-2, 1:-1]
    upper_cell = padded[:-2, 1:-1, 1:-1]
    lower_cell = padded[2:, 1:-1, 1:-1]
    vertical = upper_cell + lower_cell - 2.0 * center
    lateral = east_cell + western_neighbour + north_cell + south_cell - 4.0 * center
    change = 0.5 * east_speed * (east_cell - western_neighbour) + 0.5 * north_speed * (north_cell - south_cell)
    return wet_cells * (center + misfit + change + 0.1 * lateral + 0.15 * vertical)


def reference(adjoint_state, misfit, east_speed, north_speed, land_mask, warming_forcing_selector, vertical_filter_matrix):
    wet_cells = land_mask.astype(jnp.float32)
    current_tracer_values = adjoint_state
    for step_index in range(STEPS):
        padded = jnp.pad(current_tracer_values, ((1, 1), (1, 1), (1, 1)))
        current_tracer_values = advance(padded, misfit, east_speed, north_speed, wet_cells)
    filtered_thermal_sensitivity = jnp.einsum("cz,zne->cne", vertical_filter_matrix, current_tracer_values, precision=lax.Precision.HIGHEST)
    boundary_warming_sensitivity = warming_forcing_selector.astype(jnp.float32) * filtered_thermal_sensitivity[0]
    return filtered_thermal_sensitivity, boundary_warming_sensitivity
```

```python
import functools

import jax
import jax.numpy as jnp
from jax import lax
from jax.experimental import pallas as pl
from jax.experimental.pallas import tpu as pltpu
from jax.sharding import PartitionSpec as P

MESH = pl.DeviceIdType.MESH
SUB = 8
LANE = 128
WIDTH = 512
HIGHEST = lax.Precision.HIGHEST


def kernel(
    tiles,
    grps,
    state_ref,
    misfit_ref,
    east_ref,
    north_ref,
    land_ref,
    select_ref,
    matrix_ref,
    out_ref,
    surface_ref,
    s0,
    s1,
    s2,
    misfit,
    east,
    north,
    land,
    pencil,
    smooth,
    kron,
    load_sem,
    level_send,
    level_recv,
    row_send,
    row_recv,
    fwd_send,
    fwd_recv,
    ret_send,
    ret_recv,
):
    levels, rows, columns = state_ref.shape
    chunks = rows // SUB
    part = columns // tiles
    near = min(2, levels // 2)
    tile = lax.axis_index("tile")
    grp = lax.axis_index("grp")
    inner = (pl.ds(SUB, rows), pl.ds(LANE, columns))

    loads = [
        pltpu.make_async_copy(state_ref, s0.at[(pl.ds(1, levels),) + inner], load_sem.at[0]),
        pltpu.make_async_copy(misfit_ref, misfit, load_sem.at[1]),
        pltpu.make_async_copy(east_ref, east, load_sem.at[2]),
        pltpu.make_async_copy(north_ref, north, load_sem.at[3]),
        pltpu.make_async_copy(land_ref, land, load_sem.at[4]),
    ]
    for load in loads:
        load.start()

    barrier = pltpu.get_barrier_semaphore()

    @pl.loop(1, tiles)
    def _(i):
        other = lax.rem(tile + i, tiles)
        pl.semaphore_signal(barrier, inc=1, device_id=(grp, other), device_id_type=MESH)

    @pl.when(grp > 0)
    def _():
        pl.semaphore_signal(barrier, inc=1, device_id=(grp - 1, tile), device_id_type=MESH)

    @pl.when(grp < grps - 1)
    def _():
        pl.semaphore_signal(barrier, inc=1, device_id=(grp + 1, tile), device_id_type=MESH)

    for buf in (s0, s1):
        for start in (0, columns + LANE):
            buf[1 : levels + 1, SUB : SUB + rows, start : start + LANE] = jnp.zeros(
                (levels, rows, LANE), jnp.float32
            )

        @pl.when(tile == 0)
        def _():
            buf[0, SUB : SUB + rows, :] = jnp.zeros((rows, columns + 2 * LANE), jnp.float32)

        @pl.when(tile == tiles - 1)
        def _():
            buf[levels + 1, SUB : SUB + rows, :] = jnp.zeros((rows, columns + 2 * LANE), jnp.float32)

        @pl.when(grp == 0)
        def _():
            buf[1 : levels + 1, 0:SUB, :] = jnp.zeros((levels, SUB, columns + 2 * LANE), jnp.float32)

        @pl.when(grp == grps - 1)
        def _():
            buf[1 : levels + 1, SUB + rows :, :] = jnp.zeros(
                (levels, SUB, columns + 2 * LANE), jnp.float32
            )

    beside = (grp > 0).astype(jnp.int32) + (grp < grps - 1).astype(jnp.int32)
    pl.semaphore_wait(barrier, tiles - 1 + beside)

    def level_copies(buf, step):
        top, bottom = state_ref.at[0], state_ref.at[levels - 1]
        if step:
            top, bottom = buf.at[(1,) + inner], buf.at[(levels,) + inner]
        return [
            (
                tile > 0,
                tile < tiles - 1,
                pltpu.make_async_remote_copy(
                    top,
                    buf.at[(levels + 1,) + inner],
                    level_send.at[step, 0],
                    level_recv.at[step, 0],
                    (grp, tile - 1),
                    MESH,
                ),
            ),
            (
                tile < tiles - 1,
                tile > 0,
                pltpu.make_async_remote_copy(
                    bottom,
                    buf.at[(0,) + inner],
                    level_send.at[step, 1],
                    level_recv.at[step, 1],
                    (grp, tile + 1),
                    MESH,
                ),
            ),
        ]

    def row_copies(buf, step, slot, first, count):
        span = pl.ds(first + 1, count)
        across = pl.ds(LANE, columns)
        top, bottom = state_ref.at[:, pl.ds(0, 1), :], state_ref.at[:, pl.ds(rows - 1, 1), :]
        if step:
            top = buf.at[span, pl.ds(SUB, 1), across]
            bottom = buf.at[span, pl.ds(SUB + rows - 1, 1), across]
        return [
            (
                grp > 0,
                grp < grps - 1,
                pltpu.make_async_remote_copy(
                    top,
                    buf.at[span, pl.ds(SUB + rows, 1), across],
                    row_send.at[slot, 0],
                    row_recv.at[slot, 0],
                    (grp - 1, tile),
                    MESH,
                ),
            ),
            (
                grp < grps - 1,
                grp > 0,
                pltpu.make_async_remote_copy(
                    bottom,
                    buf.at[span, pl.ds(SUB - 1, 1), across],
                    row_send.at[slot, 1],
                    row_recv.at[slot, 1],
                    (grp + 1, tile),
                    MESH,
                ),
            ),
        ]

    def start(copies):
        for sends, _, copy in copies:
            pl.when(sends)(copy.start)

    def arrive(copies):
        for _, receives, copy in copies:
            pl.when(receives)(copy.wait_recv)

    def leave(copies):
        for sends, _, copy in copies:
            pl.when(sends)(copy.wait_send)

    sub_index = lax.broadcasted_iota(jnp.int32, (SUB, WIDTH), 0)

    def advance(src, dst, pad, first, count, row_first, row_count):
        if count <= 0:
            return

        @pl.loop(0, count * row_count)
        def _(i):
            level = first + lax.div(i, row_count)
            row = pl.multiple_of((row_first + lax.rem(i, row_count)) * SUB, SUB)
            for at in range(0, columns, WIDTH):
                here = pl.ds(at, WIDTH)
                mid = pl.ds(at + LANE, WIDTH)
                wide = src[level + 1, pl.ds(row + SUB, SUB), pl.ds(at, WIDTH + 2 * LANE)]
                center = wide[:, LANE : LANE + WIDTH]
                e = pltpu.roll(wide, WIDTH + 2 * LANE - 1, 1)[:, LANE : LANE + WIDTH]
                w = pltpu.roll(wide, 1, 1)[:, LANE : LANE + WIDTH]
                up = src[level + 1, pl.ds(row, SUB), mid]
                down = src[level + 1, pl.ds(row + 2 * SUB, SUB), mid]
                n = pltpu.roll(jnp.where(sub_index == 0, down, center), SUB - 1, 0)
                s = pltpu.roll(jnp.where(sub_index == SUB - 1, up, center), 1, 0)
                a = src[level, pl.ds(row + SUB, SUB), mid]
                b = src[level + 2, pl.ds(row + SUB, SUB), mid]
                rr = pl.ds(row, SUB)
                flow = east[level, rr, here] * (e - w) + north[level, rr, here] * (n - s)
                value = (
                    (0.3 * center + misfit[level, rr, here])
                    + 0.5 * flow
                    + (0.1 * ((e + w) + (n + s)) + 0.15 * (a + b))
                )
                value = land[level, rr, here].astype(jnp.float32) * value
                if pad:
                    dst[level + 1, pl.ds(row + SUB, SUB), mid] = value
                else:
                    dst[level, rr, here] = value

    def forward(first, count, row_first, row_count):
        if count <= 0:
            return
        for r in range(row_first, row_first + row_count):
            span = pl.ds(r * SUB, SUB)
            target = pencil.at[pl.ds(tile * levels + first, count), span, :]

            @pl.loop(1, tiles)
            def _(i):
                other = lax.rem(tile + i, tiles)
                mine = pl.ds(pl.multiple_of(other * part, LANE), part)
                pltpu.make_async_remote_copy(
                    s2.at[pl.ds(first, count), span, mine],
                    target,
                    fwd_send,
                    fwd_recv.at[r],
                    (grp, other),
                    MESH,
                ).start()

            own = pl.ds(pl.multiple_of(tile * part, LANE), part)
            pltpu.make_async_copy(
                s2.at[pl.ds(first, count), span, own], target, fwd_recv.at[r]
            ).start()

    level0 = level_copies(s0, 0)
    row0 = row_copies(s0, 0, 0, 0, levels)
    start(row0)
    start(level0)
    for load in loads:
        load.wait()
    arrive(row0)

    advance(s0, s1, True, 1, levels - 2, 0, chunks)
    level1 = level_copies(s1, 1)
    row_mid = row_copies(s1, 1, 1, 1, levels - 2) if levels > 2 else []
    row_ends = row_copies(s1, 1, 2, 0, 1) + row_copies(s1, 1, 3, levels - 1, 1)
    start(row_mid)

    early = levels - 2 * near
    advance(s1, s2, False, near, early, 1, chunks - 2)
    forward(near, early, 1, chunks - 2)

    arrive(level0)
    advance(s0, s1, True, 0, 1, 0, chunks)
    advance(s0, s1, True, levels - 1, 1, 0, chunks)
    start(level1)
    start(row_ends)

    arrive(row_mid)
    for r in (0, chunks - 1):
        advance(s1, s2, False, near, early, r, 1)
        forward(near, early, r, 1)
    advance(s1, s2, False, 1, near - 1, 0, chunks)
    advance(s1, s2, False, levels - near, near - 1, 0, chunks)

    size = tiles * levels * SUB
    repeat = (
        lax.shift_right_logical(lax.broadcasted_iota(jnp.int32, (size, tiles * levels), 0), 3)
        == lax.broadcasted_iota(jnp.int32, (size, tiles * levels), 1)
    ).astype(jnp.float32)
    tall = jnp.dot(repeat, matrix_ref[...], precision=HIGHEST, preferred_element_type=jnp.float32)
    full = lax.dot_general(
        tall,
        repeat,
        (((1,), (1,)), ((), ())),
        precision=HIGHEST,
        preferred_element_type=jnp.float32,
    )
    same = (lax.broadcasted_iota(jnp.int32, (size, size), 0) & (SUB - 1)) == (
        lax.broadcasted_iota(jnp.int32, (size, size), 1) & (SUB - 1)
    )
    kron[...] = jnp.where(same, full, 0.0)

    arrive(level1)
    arrive(row_ends)
    order = list(range(1, chunks - 1)) + [0, chunks - 1]
    for r in order:
        advance(s1, s2, False, 0, 1, r, 1)
        advance(s1, s2, False, levels - 1, 1, r, 1)
        forward(0, near, r, 1)
        forward(levels - near, near, r, 1)

    for r in order:
        span = pl.ds(r * SUB, SUB)
        chunk = pencil.at[:, span, :]
        pltpu.make_async_copy(chunk, chunk, fwd_recv.at[r]).wait()
        result = jnp.dot(
            kron[...],
            pencil[:, r * SUB : (r + 1) * SUB, :].reshape(size, part),
            precision=HIGHEST,
            preferred_element_type=jnp.float32,
        )
        smooth[:, r * SUB : (r + 1) * SUB, :] = result.reshape(tiles * levels, SUB, part)
        home = out_ref.at[:, span, pl.ds(pl.multiple_of(tile * part, LANE), part)]

        @pl.loop(1, tiles)
        def _(i):
            other = lax.rem(tile + i, tiles)
            pltpu.make_async_remote_copy(
                smooth.at[pl.ds(other * levels, levels), span, :],
                home,
                ret_send,
                ret_recv,
                (grp, other),
                MESH,
            ).start()

        pltpu.make_async_copy(
            smooth.at[pl.ds(tile * levels, levels), span, :], home, ret_recv
        ).start()
        surface_ref[r * SUB : (r + 1) * SUB, :] = (
            select_ref[r * SUB : (r + 1) * SUB, :].astype(jnp.float32) * result[0:SUB]
        )

    for copies in (level0, row0, level1, row_mid, row_ends):
        leave(copies)
    sent = s2.at[:, :, pl.ds(0, (tiles - 1) * part)]
    pltpu.make_async_copy(sent, sent, fwd_send).wait()
    returned = smooth.at[pl.ds(0, (tiles - 1) * levels)]
    pltpu.make_async_copy(returned, returned, ret_send).wait()
    pltpu.make_async_copy(out_ref, out_ref, ret_recv).wait()


def body(tiles, grps, *args):
    levels, rows, columns = args[0].shape
    part = columns // tiles
    total = tiles * levels
    padded = (levels + 2, rows + 2 * SUB, columns + 2 * LANE)
    block = (levels, rows, columns)
    anywhere = pl.BlockSpec(memory_space=pl.ANY)
    vmem = pl.BlockSpec(memory_space=pltpu.VMEM)
    return pl.pallas_call(
        functools.partial(kernel, tiles, grps),
        out_shape=(
            jax.ShapeDtypeStruct(block, jnp.float32),
            jax.ShapeDtypeStruct((rows, part), jnp.float32),
        ),
        in_specs=[anywhere] * 5 + [vmem] * 2,
        out_specs=(anywhere, vmem),
        scratch_shapes=[
            pltpu.VMEM(padded, jnp.float32),
            pltpu.VMEM(padded, jnp.float32),
            pltpu.VMEM(block, jnp.float32),
            pltpu.VMEM(block, jnp.float32),
            pltpu.VMEM(block, jnp.float32),
            pltpu.VMEM(block, jnp.float32),
            pltpu.VMEM(block, jnp.int32),
            pltpu.VMEM((total, rows, part), jnp.float32),
            pltpu.VMEM((total, rows, part), jnp.float32),
            pltpu.VMEM((total * SUB, total * SUB), jnp.float32),
            pltpu.SemaphoreType.DMA((5,)),
            pltpu.SemaphoreType.DMA((2, 2)),
            pltpu.SemaphoreType.DMA((2, 2)),
            pltpu.SemaphoreType.DMA((4, 2)),
            pltpu.SemaphoreType.DMA((4, 2)),
            pltpu.SemaphoreType.DMA,
            pltpu.SemaphoreType.DMA((rows // SUB,)),
            pltpu.SemaphoreType.DMA,
            pltpu.SemaphoreType.DMA,
        ],
        compiler_params=pltpu.CompilerParams(
            collective_id=0, has_side_effects=True, vmem_limit_bytes=56 * 1024 * 1024
        ),
    )(*args)


def solution(mesh):
    split = P("tile", "grp", None)
    return jax.shard_map(
        functools.partial(body, mesh.shape["tile"], mesh.shape["grp"]),
        mesh=mesh,
        in_specs=(split,) * 5 + (P("grp", "tile"), P()),
        out_specs=(split, P("grp", "tile")),
        check_vma=False,
    )
```

```python
import functools

import jax
import jax.numpy as jnp
from jax import lax
from jax.experimental import pallas as pl
from jax.experimental.pallas import tpu as pltpu
from jax.sharding import PartitionSpec as P

MESH = pl.DeviceIdType.MESH
SUB = 8
LANE = 128
WIDTH = 512
HIGHEST = lax.Precision.HIGHEST


def kernel(
    tiles,
    grps,
    state_ref,
    misfit_ref,
    east_ref,
    north_ref,
    land_ref,
    matrix_ref,
    out_ref,
    surface_ref,
    s0,
    s1,
    s2,
    misfit,
    east,
    north,
    land,
    pencil,
    smooth,
    kron,
    load_sem,
    level_send,
    level_recv,
    row_send,
    row_recv,
    fwd_send,
    fwd_recv,
    ret_send,
    ret_recv,
):
    levels, rows, columns = state_ref.shape
    chunks = rows // SUB
    part = columns // tiles
    near = min(2, levels // 2)
    tile = lax.axis_index("tile")
    grp = lax.axis_index("grp")
    inner = (pl.ds(SUB, rows), pl.ds(LANE, columns))

    loads = [
        pltpu.make_async_copy(state_ref, s0.at[(pl.ds(1, levels),) + inner], load_sem.at[0]),
        pltpu.make_async_copy(misfit_ref, misfit, load_sem.at[1]),
        pltpu.make_async_copy(east_ref, east, load_sem.at[2]),
        pltpu.make_async_copy(north_ref, north, load_sem.at[3]),
        pltpu.make_async_copy(land_ref, land, load_sem.at[4]),
    ]
    for load in loads:
        load.start()

    barrier = pltpu.get_barrier_semaphore()

    @pl.loop(1, tiles)
    def _(i):
        other = lax.rem(tile + i, tiles)
        pl.semaphore_signal(barrier, inc=1, device_id=(grp, other), device_id_type=MESH)

    @pl.when(grp > 0)
    def _():
        pl.semaphore_signal(barrier, inc=1, device_id=(grp - 1, tile), device_id_type=MESH)

    @pl.when(grp < grps - 1)
    def _():
        pl.semaphore_signal(barrier, inc=1, device_id=(grp + 1, tile), device_id_type=MESH)

    for buf in (s0, s1):
        for start in (0, columns + LANE):
            buf[1 : levels + 1, SUB : SUB + rows, start : start + LANE] = jnp.zeros(
                (levels, rows, LANE), jnp.float32
            )

        @pl.when(tile == 0)
        def _():
            buf[0, SUB : SUB + rows, :] = jnp.zeros((rows, columns + 2 * LANE), jnp.float32)

        @pl.when(tile == tiles - 1)
        def _():
            buf[levels + 1, SUB : SUB + rows, :] = jnp.zeros((rows, columns + 2 * LANE), jnp.float32)

        @pl.when(grp == 0)
        def _():
            buf[1 : levels + 1, 0:SUB, :] = jnp.zeros((levels, SUB, columns + 2 * LANE), jnp.float32)

        @pl.when(grp == grps - 1)
        def _():
            buf[1 : levels + 1, SUB + rows :, :] = jnp.zeros(
                (levels, SUB, columns + 2 * LANE), jnp.float32
            )

    beside = (grp > 0).astype(jnp.int32) + (grp < grps - 1).astype(jnp.int32)
    pl.semaphore_wait(barrier, tiles - 1 + beside)

    def level_copies(buf, step):
        top, bottom = state_ref.at[0], state_ref.at[levels - 1]
        if step:
            top, bottom = buf.at[(1,) + inner], buf.at[(levels,) + inner]
        return [
            (
                tile > 0,
                tile < tiles - 1,
                pltpu.make_async_remote_copy(
                    top,
                    buf.at[(levels + 1,) + inner],
                    level_send.at[step, 0],
                    level_recv.at[step, 0],
                    (grp, tile - 1),
                    MESH,
                ),
            ),
            (
                tile < tiles - 1,
                tile > 0,
                pltpu.make_async_remote_copy(
                    bottom,
                    buf.at[(0,) + inner],
                    level_send.at[step, 1],
                    level_recv.at[step, 1],
                    (grp, tile + 1),
                    MESH,
                ),
            ),
        ]

    def row_copies(buf, step, slot, first, count):
        span = pl.ds(first + 1, count)
        across = pl.ds(LANE, columns)
        top, bottom = state_ref.at[:, pl.ds(0, 1), :], state_ref.at[:, pl.ds(rows - 1, 1), :]
        if step:
            top = buf.at[span, pl.ds(SUB, 1), across]
            bottom = buf.at[span, pl.ds(SUB + rows - 1, 1), across]
        return [
            (
                grp > 0,
                grp < grps - 1,
                pltpu.make_async_remote_copy(
                    top,
                    buf.at[span, pl.ds(SUB + rows, 1), across],
                    row_send.at[slot, 0],
                    row_recv.at[slot, 0],
                    (grp - 1, tile),
                    MESH,
                ),
            ),
            (
                grp < grps - 1,
                grp > 0,
                pltpu.make_async_remote_copy(
                    bottom,
                    buf.at[span, pl.ds(SUB - 1, 1), across],
                    row_send.at[slot, 1],
                    row_recv.at[slot, 1],
                    (grp + 1, tile),
                    MESH,
                ),
            ),
        ]

    def start(copies):
        for sends, _, copy in copies:
            pl.when(sends)(copy.start)

    def arrive(copies):
        for _, receives, copy in copies:
            pl.when(receives)(copy.wait_recv)

    def leave(copies):
        for sends, _, copy in copies:
            pl.when(sends)(copy.wait_send)

    sub_index = lax.broadcasted_iota(jnp.int32, (SUB, WIDTH), 0)

    def advance(src, dst, pad, first, count, row_first, row_count):
        if count <= 0:
            return

        @pl.loop(0, count * row_count)
        def _(i):
            level = first + lax.div(i, row_count)
            row = pl.multiple_of((row_first + lax.rem(i, row_count)) * SUB, SUB)
            for at in range(0, columns, WIDTH):
                here = pl.ds(at, WIDTH)
                mid = pl.ds(at + LANE, WIDTH)
                wide = src[level + 1, pl.ds(row + SUB, SUB), pl.ds(at, WIDTH + 2 * LANE)]
                center = wide[:, LANE : LANE + WIDTH]
                e = pltpu.roll(wide, WIDTH + 2 * LANE - 1, 1)[:, LANE : LANE + WIDTH]
                w = pltpu.roll(wide, 1, 1)[:, LANE : LANE + WIDTH]
                up = src[level + 1, pl.ds(row, SUB), mid]
                down = src[level + 1, pl.ds(row + 2 * SUB, SUB), mid]
                n = pltpu.roll(jnp.where(sub_index == 0, down, center), SUB - 1, 0)
                s = pltpu.roll(jnp.where(sub_index == SUB - 1, up, center), 1, 0)
                a = src[level, pl.ds(row + SUB, SUB), mid]
                b = src[level + 2, pl.ds(row + SUB, SUB), mid]
                rr = pl.ds(row, SUB)
                flow = east[level, rr, here] * (e - w) + north[level, rr, here] * (n - s)
                value = (
                    (0.3 * center + misfit[level, rr, here])
                    + 0.5 * flow
                    + (0.1 * ((e + w) + (n + s)) + 0.15 * (a + b))
                )
                value = land[level, rr, here].astype(jnp.float32) * value
                if pad:
                    dst[level + 1, pl.ds(row + SUB, SUB), mid] = value
                else:
                    dst[level, rr, here] = value

    def forward(first, count, row_first, row_count):
        if count <= 0:
            return
        for r in range(row_first, row_first + row_count):
            span = pl.ds(r * SUB, SUB)
            target = pencil.at[pl.ds(tile * levels + first, count), span, :]

            @pl.loop(1, tiles)
            def _(i):
                other = lax.rem(tile + i, tiles)
                mine = pl.ds(pl.multiple_of(other * part, LANE), part)
                pltpu.make_async_remote_copy(
                    s2.at[pl.ds(first, count), span, mine],
                    target,
                    fwd_send,
                    fwd_recv.at[r],
                    (grp, other),
                    MESH,
                ).start()

            own = pl.ds(pl.multiple_of(tile * part, LANE), part)
            pltpu.make_async_copy(
                s2.at[pl.ds(first, count), span, own], target, fwd_recv.at[r]
            ).start()

    level0 = level_copies(s0, 0)
    row0 = row_copies(s0, 0, 0, 0, levels)
    start(row0)
    start(level0)
    for load in loads:
        load.wait()

    level1 = level_copies(s1, 1)
    row_mid = row_copies(s1, 1, 1, 1, levels - 2) if levels > 2 else []
    row_ends = row_copies(s1, 1, 2, 0, 1) + row_copies(s1, 1, 3, levels - 1, 1)
    early = levels - 2 * near
    middle = chunks - 2
    advance(s0, s1, True, 1, levels - 2, 1, middle)
    arrive(row0)
    advance(s0, s1, True, 1, levels - 2, 0, 1)
    for r in range(1, middle):
        advance(s1, s2, False, near, early, r, 1)
        forward(near, early, r, 1)
    advance(s0, s1, True, 1, levels - 2, chunks - 1, 1)
    start(row_mid)
    arrive(level0)
    advance(s0, s1, True, 0, 1, 0, chunks)
    advance(s0, s1, True, levels - 1, 1, 0, chunks)
    start(level1)
    start(row_ends)
    advance(s1, s2, False, near, early, middle, 1)
    forward(near, early, middle, 1)

    arrive(row_mid)
    for r in (0, chunks - 1):
        advance(s1, s2, False, near, early, r, 1)
        forward(near, early, r, 1)
    advance(s1, s2, False, 1, near - 1, 0, chunks)
    advance(s1, s2, False, levels - near, near - 1, 0, chunks)

    arrive(level1)
    arrive(row_ends)
    order = list(range(1, chunks - 1)) + [0, chunks - 1]
    for r in order:
        advance(s1, s2, False, 0, 1, r, 1)
        advance(s1, s2, False, levels - 1, 1, r, 1)
        forward(0, near, r, 1)
        forward(levels - near, near, r, 1)

    size = tiles * levels * SUB
    repeat = (
        lax.shift_right_logical(lax.broadcasted_iota(jnp.int32, (size, tiles * levels), 0), 3)
        == lax.broadcasted_iota(jnp.int32, (size, tiles * levels), 1)
    ).astype(jnp.float32)
    tall = jnp.dot(repeat, matrix_ref[...], precision=HIGHEST, preferred_element_type=jnp.float32)
    full = lax.dot_general(
        tall,
        repeat,
        (((1,), (1,)), ((), ())),
        precision=HIGHEST,
        preferred_element_type=jnp.float32,
    )
    same = (lax.broadcasted_iota(jnp.int32, (size, size), 0) & (SUB - 1)) == (
        lax.broadcasted_iota(jnp.int32, (size, size), 1) & (SUB - 1)
    )
    kron[...] = jnp.where(same, full, 0.0)

    for r in order:
        span = pl.ds(r * SUB, SUB)
        chunk = pencil.at[:, span, :]
        pltpu.make_async_copy(chunk, chunk, fwd_recv.at[r]).wait()
        result = jnp.dot(
            kron[...],
            pencil[:, r * SUB : (r + 1) * SUB, :].reshape(size, part),
            precision=HIGHEST,
            preferred_element_type=jnp.float32,
        )
        smooth[:, r * SUB : (r + 1) * SUB, :] = result.reshape(tiles * levels, SUB, part)
        home = out_ref.at[:, span, pl.ds(pl.multiple_of(tile * part, LANE), part)]

        @pl.loop(1, tiles)
        def _(i):
            other = lax.rem(tile + i, tiles)
            pltpu.make_async_remote_copy(
                smooth.at[pl.ds(other * levels, levels), span, :],
                home,
                ret_send,
                ret_recv,
                (grp, other),
                MESH,
            ).start()

        pltpu.make_async_copy(
            smooth.at[pl.ds(tile * levels, levels), span, :], home, ret_recv
        ).start()
        surface_ref[r * SUB : (r + 1) * SUB, :] = result[0:SUB]

    for copies in (level0, row0, level1, row_mid, row_ends):
        leave(copies)
    sent = s2.at[:, :, pl.ds(0, (tiles - 1) * part)]
    pltpu.make_async_copy(sent, sent, fwd_send).wait()
    returned = smooth.at[pl.ds(0, (tiles - 1) * levels)]
    pltpu.make_async_copy(returned, returned, ret_send).wait()
    pltpu.make_async_copy(out_ref, out_ref, ret_recv).wait()


def body(tiles, grps, *args):
    args, select = args[:5] + args[6:], args[5]
    levels, rows, columns = args[0].shape
    part = columns // tiles
    total = tiles * levels
    padded = (levels + 2, rows + 2 * SUB, columns + 2 * LANE)
    block = (levels, rows, columns)
    anywhere = pl.BlockSpec(memory_space=pl.ANY)
    vmem = pl.BlockSpec(memory_space=pltpu.VMEM)
    filtered, surface = pl.pallas_call(
        functools.partial(kernel, tiles, grps),
        out_shape=(
            jax.ShapeDtypeStruct(block, jnp.float32),
            jax.ShapeDtypeStruct((rows, part), jnp.float32),
        ),
        in_specs=[anywhere] * 5 + [vmem],
        out_specs=(anywhere, vmem),
        scratch_shapes=[
            pltpu.VMEM(padded, jnp.float32),
            pltpu.VMEM(padded, jnp.float32),
            pltpu.VMEM(block, jnp.float32),
            pltpu.VMEM(block, jnp.float32),
            pltpu.VMEM(block, jnp.float32),
            pltpu.VMEM(block, jnp.float32),
            pltpu.VMEM(block, jnp.int32),
            pltpu.VMEM((total, rows, part), jnp.float32),
            pltpu.VMEM((total, rows, part), jnp.float32),
            pltpu.VMEM((total * SUB, total * SUB), jnp.float32),
            pltpu.SemaphoreType.DMA((5,)),
            pltpu.SemaphoreType.DMA((2, 2)),
            pltpu.SemaphoreType.DMA((2, 2)),
            pltpu.SemaphoreType.DMA((4, 2)),
            pltpu.SemaphoreType.DMA((4, 2)),
            pltpu.SemaphoreType.DMA,
            pltpu.SemaphoreType.DMA((rows // SUB,)),
            pltpu.SemaphoreType.DMA,
            pltpu.SemaphoreType.DMA,
        ],
        compiler_params=pltpu.CompilerParams(
            collective_id=0, has_side_effects=True, vmem_limit_bytes=56 * 1024 * 1024
        ),
    )(*args)
    return filtered, select.astype(jnp.float32) * surface


def solution(mesh):
    split = P("tile", "grp", None)
    return jax.shard_map(
        functools.partial(body, mesh.shape["tile"], mesh.shape["grp"]),
        mesh=mesh,
        in_specs=(split,) * 5 + (P("grp", "tile"), P()),
        out_specs=(split, P("grp", "tile")),
        check_vma=False,
    )
```

```python
import functools

import jax
import jax.numpy as jnp
from jax import lax
from jax.experimental import pallas as pl
from jax.experimental.pallas import tpu as pltpu
from jax.sharding import PartitionSpec as P

MESH = pl.DeviceIdType.MESH
SUB = 8
LANE = 128
WIDTH = 512
HIGHEST = lax.Precision.HIGHEST


def kernel(
    tiles,
    grps,
    state_ref,
    misfit_ref,
    east_ref,
    north_ref,
    land_ref,
    matrix_ref,
    out_ref,
    surface_ref,
    s0,
    s1,
    s2,
    misfit,
    east,
    north,
    land,
    pencil,
    smooth,
    kron,
    load_sem,
    level_send,
    level_recv,
    row_send,
    row_recv,
    fwd_send,
    fwd_recv,
    ret_send,
    ret_recv,
):
    levels, rows, columns = state_ref.shape
    chunks = rows // SUB
    part = columns // tiles
    near = min(2, levels // 2)
    tile = lax.axis_index("tile")
    grp = lax.axis_index("grp")
    inner = (pl.ds(SUB, rows), pl.ds(LANE, columns))

    loads = [
        pltpu.make_async_copy(state_ref, s0.at[(pl.ds(1, levels),) + inner], load_sem.at[0]),
        pltpu.make_async_copy(misfit_ref, misfit, load_sem.at[1]),
        pltpu.make_async_copy(east_ref, east, load_sem.at[2]),
        pltpu.make_async_copy(north_ref, north, load_sem.at[3]),
        pltpu.make_async_copy(land_ref, land, load_sem.at[4]),
    ]
    for load in loads:
        load.start()

    barrier = pltpu.get_barrier_semaphore()

    @pl.loop(1, tiles)
    def _(i):
        other = lax.rem(tile + i, tiles)
        pl.semaphore_signal(barrier, inc=1, device_id=(grp, other), device_id_type=MESH)

    @pl.when(grp > 0)
    def _():
        pl.semaphore_signal(barrier, inc=1, device_id=(grp - 1, tile), device_id_type=MESH)

    @pl.when(grp < grps - 1)
    def _():
        pl.semaphore_signal(barrier, inc=1, device_id=(grp + 1, tile), device_id_type=MESH)

    for buf in (s0, s1):
        for start in (0, columns + LANE):
            buf[1 : levels + 1, SUB : SUB + rows, start : start + LANE] = jnp.zeros(
                (levels, rows, LANE), jnp.float32
            )

        @pl.when(tile == 0)
        def _():
            buf[0, SUB : SUB + rows, :] = jnp.zeros((rows, columns + 2 * LANE), jnp.float32)

        @pl.when(tile == tiles - 1)
        def _():
            buf[levels + 1, SUB : SUB + rows, :] = jnp.zeros((rows, columns + 2 * LANE), jnp.float32)

        @pl.when(grp == 0)
        def _():
            buf[1 : levels + 1, 0:SUB, :] = jnp.zeros((levels, SUB, columns + 2 * LANE), jnp.float32)

        @pl.when(grp == grps - 1)
        def _():
            buf[1 : levels + 1, SUB + rows :, :] = jnp.zeros(
                (levels, SUB, columns + 2 * LANE), jnp.float32
            )

    beside = (grp > 0).astype(jnp.int32) + (grp < grps - 1).astype(jnp.int32)
    pl.semaphore_wait(barrier, tiles - 1 + beside)

    def level_copies(buf, step):
        top, bottom = state_ref.at[0], state_ref.at[levels - 1]
        if step:
            top, bottom = buf.at[(1,) + inner], buf.at[(levels,) + inner]
        return [
            (
                tile > 0,
                tile < tiles - 1,
                pltpu.make_async_remote_copy(
                    top,
                    buf.at[(levels + 1,) + inner],
                    level_send.at[step, 0],
                    level_recv.at[step, 0],
                    (grp, tile - 1),
                    MESH,
                ),
            ),
            (
                tile < tiles - 1,
                tile > 0,
                pltpu.make_async_remote_copy(
                    bottom,
                    buf.at[(0,) + inner],
                    level_send.at[step, 1],
                    level_recv.at[step, 1],
                    (grp, tile + 1),
                    MESH,
                ),
            ),
        ]

    def row_copies(buf, step, slot, first, count):
        span = pl.ds(first + 1, count)
        across = pl.ds(LANE, columns)
        top, bottom = state_ref.at[:, pl.ds(0, 1), :], state_ref.at[:, pl.ds(rows - 1, 1), :]
        if step:
            top = buf.at[span, pl.ds(SUB, 1), across]
            bottom = buf.at[span, pl.ds(SUB + rows - 1, 1), across]
        return [
            (
                grp > 0,
                grp < grps - 1,
                pltpu.make_async_remote_copy(
                    top,
                    buf.at[span, pl.ds(SUB + rows, 1), across],
                    row_send.at[slot, 0],
                    row_recv.at[slot, 0],
                    (grp - 1, tile),
                    MESH,
                ),
            ),
            (
                grp < grps - 1,
                grp > 0,
                pltpu.make_async_remote_copy(
                    bottom,
                    buf.at[span, pl.ds(SUB - 1, 1), across],
                    row_send.at[slot, 1],
                    row_recv.at[slot, 1],
                    (grp + 1, tile),
                    MESH,
                ),
            ),
        ]

    def start(copies):
        for sends, _, copy in copies:
            pl.when(sends)(copy.start)

    def arrive(copies):
        for _, receives, copy in copies:
            pl.when(receives)(copy.wait_recv)

    def leave(copies):
        for sends, _, copy in copies:
            pl.when(sends)(copy.wait_send)

    sub_index = lax.broadcasted_iota(jnp.int32, (SUB, WIDTH), 0)

    def advance(src, dst, pad, first, count, row_first, row_count):
        if count <= 0:
            return

        @pl.loop(0, count * row_count)
        def _(i):
            level = first + lax.div(i, row_count)
            row = pl.multiple_of((row_first + lax.rem(i, row_count)) * SUB, SUB)
            for at in range(0, columns, WIDTH):
                here = pl.ds(at, WIDTH)
                mid = pl.ds(at + LANE, WIDTH)
                wide = src[level + 1, pl.ds(row + SUB, SUB), pl.ds(at, WIDTH + 2 * LANE)]
                center = wide[:, LANE : LANE + WIDTH]
                e = pltpu.roll(wide, WIDTH + 2 * LANE - 1, 1)[:, LANE : LANE + WIDTH]
                w = pltpu.roll(wide, 1, 1)[:, LANE : LANE + WIDTH]
                up = src[level + 1, pl.ds(row, SUB), mid]
                down = src[level + 1, pl.ds(row + 2 * SUB, SUB), mid]
                n = pltpu.roll(jnp.where(sub_index == 0, down, center), SUB - 1, 0)
                s = pltpu.roll(jnp.where(sub_index == SUB - 1, up, center), 1, 0)
                a = src[level, pl.ds(row + SUB, SUB), mid]
                b = src[level + 2, pl.ds(row + SUB, SUB), mid]
                rr = pl.ds(row, SUB)
                flow = east[level, rr, here] * (e - w) + north[level, rr, here] * (n - s)
                value = (
                    (0.3 * center + misfit[level, rr, here])
                    + 0.5 * flow
                    + (0.1 * ((e + w) + (n + s)) + 0.15 * (a + b))
                )
                value = land[level, rr, here].astype(jnp.float32) * value
                if pad:
                    dst[level + 1, pl.ds(row + SUB, SUB), mid] = value
                else:
                    dst[level, rr, here] = value

    def forward(first, count, row_first, row_count):
        if count <= 0:
            return
        for r in range(row_first, row_first + row_count):
            span = pl.ds(r * SUB, SUB)
            target = pencil.at[pl.ds(tile * levels + first, count), span, :]

            @pl.loop(1, tiles)
            def _(i):
                other = lax.rem(tile + i, tiles)
                mine = pl.ds(pl.multiple_of(other * part, LANE), part)
                pltpu.make_async_remote_copy(
                    s2.at[pl.ds(first, count), span, mine],
                    target,
                    fwd_send,
                    fwd_recv.at[r],
                    (grp, other),
                    MESH,
                ).start()

            own = pl.ds(pl.multiple_of(tile * part, LANE), part)
            pltpu.make_async_copy(
                s2.at[pl.ds(first, count), span, own], target, fwd_recv.at[r]
            ).start()

    level0 = level_copies(s0, 0)
    row0 = row_copies(s0, 0, 0, 0, levels)
    start(row0)
    start(level0)
    for load in loads:
        load.wait()
    arrive(row0)

    advance(s0, s1, True, 1, levels - 2, 0, chunks)
    level1 = level_copies(s1, 1)
    row_mid = row_copies(s1, 1, 1, 1, levels - 2) if levels > 2 else []
    row_ends = row_copies(s1, 1, 2, 0, 1) + row_copies(s1, 1, 3, levels - 1, 1)
    start(row_mid)

    early = levels - 2 * near
    advance(s1, s2, False, near, early, 1, chunks - 2)
    forward(near, early, 1, chunks - 2)

    arrive(row_mid)
    for r in (0, chunks - 1):
        advance(s1, s2, False, near, early, r, 1)
        forward(near, early, r, 1)

    arrive(level0)
    advance(s0, s1, True, 0, 1, 0, chunks)
    advance(s0, s1, True, levels - 1, 1, 0, chunks)
    start(level1)
    start(row_ends)
    advance(s1, s2, False, 1, near - 1, 0, chunks)
    advance(s1, s2, False, levels - near, near - 1, 0, chunks)

    size = tiles * levels * SUB
    repeat = (
        lax.shift_right_logical(lax.broadcasted_iota(jnp.int32, (size, tiles * levels), 0), 3)
        == lax.broadcasted_iota(jnp.int32, (size, tiles * levels), 1)
    ).astype(jnp.float32)
    tall = jnp.dot(repeat, matrix_ref[...], precision=HIGHEST, preferred_element_type=jnp.float32)
    full = lax.dot_general(
        tall,
        repeat,
        (((1,), (1,)), ((), ())),
        precision=HIGHEST,
        preferred_element_type=jnp.float32,
    )
    same = (lax.broadcasted_iota(jnp.int32, (size, size), 0) & (SUB - 1)) == (
        lax.broadcasted_iota(jnp.int32, (size, size), 1) & (SUB - 1)
    )
    kron[...] = jnp.where(same, full, 0.0)

    arrive(level1)
    arrive(row_ends)
    order = list(range(1, chunks - 1)) + [0, chunks - 1]
    for r in order:
        advance(s1, s2, False, 0, 1, r, 1)
        advance(s1, s2, False, levels - 1, 1, r, 1)
        forward(0, near, r, 1)
        forward(levels - near, near, r, 1)

    for r in order:
        span = pl.ds(r * SUB, SUB)
        chunk = pencil.at[:, span, :]
        pltpu.make_async_copy(chunk, chunk, fwd_recv.at[r]).wait()
        result = jnp.dot(
            kron[...],
            pencil[:, r * SUB : (r + 1) * SUB, :].reshape(size, part),
            precision=HIGHEST,
            preferred_element_type=jnp.float32,
        )
        smooth[:, r * SUB : (r + 1) * SUB, :] = result.reshape(tiles * levels, SUB, part)
        home = out_ref.at[:, span, pl.ds(pl.multiple_of(tile * part, LANE), part)]

        @pl.loop(1, tiles)
        def _(i):
            other = lax.rem(tile + i, tiles)
            pltpu.make_async_remote_copy(
                smooth.at[pl.ds(other * levels, levels), span, :],
                home,
                ret_send,
                ret_recv,
                (grp, other),
                MESH,
            ).start()

        pltpu.make_async_copy(
            smooth.at[pl.ds(tile * levels, levels), span, :], home, ret_recv
        ).start()
        surface_ref[r * SUB : (r + 1) * SUB, :] = result[0:SUB]

    for copies in (level0, row0, level1, row_mid, row_ends):
        leave(copies)
    sent = s2.at[:, :, pl.ds(0, (tiles - 1) * part)]
    pltpu.make_async_copy(sent, sent, fwd_send).wait()
    returned = smooth.at[pl.ds(0, (tiles - 1) * levels)]
    pltpu.make_async_copy(returned, returned, ret_send).wait()
    pltpu.make_async_copy(out_ref, out_ref, ret_recv).wait()


def body(tiles, grps, *args):
    args, select = args[:5] + args[6:], args[5]
    levels, rows, columns = args[0].shape
    part = columns // tiles
    total = tiles * levels
    padded = (levels + 2, rows + 2 * SUB, columns + 2 * LANE)
    block = (levels, rows, columns)
    anywhere = pl.BlockSpec(memory_space=pl.ANY)
    vmem = pl.BlockSpec(memory_space=pltpu.VMEM)
    filtered, surface = pl.pallas_call(
        functools.partial(kernel, tiles, grps),
        out_shape=(
            jax.ShapeDtypeStruct(block, jnp.float32),
            jax.ShapeDtypeStruct((rows, part), jnp.float32),
        ),
        in_specs=[anywhere] * 5 + [vmem],
        out_specs=(anywhere, vmem),
        scratch_shapes=[
            pltpu.VMEM(padded, jnp.float32),
            pltpu.VMEM(padded, jnp.float32),
            pltpu.VMEM(block, jnp.float32),
            pltpu.VMEM(block, jnp.float32),
            pltpu.VMEM(block, jnp.float32),
            pltpu.VMEM(block, jnp.float32),
            pltpu.VMEM(block, jnp.int32),
            pltpu.VMEM((total, rows, part), jnp.float32),
            pltpu.VMEM((total, rows, part), jnp.float32),
            pltpu.VMEM((total * SUB, total * SUB), jnp.float32),
            pltpu.SemaphoreType.DMA((5,)),
            pltpu.SemaphoreType.DMA((2, 2)),
            pltpu.SemaphoreType.DMA((2, 2)),
            pltpu.SemaphoreType.DMA((4, 2)),
            pltpu.SemaphoreType.DMA((4, 2)),
            pltpu.SemaphoreType.DMA,
            pltpu.SemaphoreType.DMA((rows // SUB,)),
            pltpu.SemaphoreType.DMA,
            pltpu.SemaphoreType.DMA,
        ],
        compiler_params=pltpu.CompilerParams(
            collective_id=0, has_side_effects=True, vmem_limit_bytes=56 * 1024 * 1024
        ),
    )(*args)
    return filtered, select.astype(jnp.float32) * surface


def solution(mesh):
    split = P("tile", "grp", None)
    return jax.shard_map(
        functools.partial(body, mesh.shape["tile"], mesh.shape["grp"]),
        mesh=mesh,
        in_specs=(split,) * 5 + (P("grp", "tile"), P()),
        out_specs=(split, P("grp", "tile")),
        check_vma=False,
    )
```

```python
import functools

import jax
import jax.numpy as jnp
from jax import lax
from jax.experimental import pallas as pl
from jax.experimental.pallas import tpu as pltpu
from jax.sharding import PartitionSpec as P

MESH = pl.DeviceIdType.MESH
SUB = 8
LANE = 128
WIDTH = 512
HIGHEST = lax.Precision.HIGHEST


def kernel(
    tiles,
    grps,
    state_ref,
    misfit_ref,
    east_ref,
    north_ref,
    land_ref,
    matrix_ref,
    out_ref,
    surface_ref,
    s0,
    s1,
    s2,
    misfit,
    east,
    north,
    land,
    pencil,
    smooth,
    kron,
    load_sem,
    level_send,
    level_recv,
    row_send,
    row_recv,
    fwd_send,
    fwd_recv,
    ret_send,
    ret_recv,
):
    levels, rows, columns = state_ref.shape
    chunks = rows // SUB
    part = columns // tiles
    near = min(2, levels // 2)
    tile = lax.axis_index("tile")
    grp = lax.axis_index("grp")
    inner = (pl.ds(SUB, rows), pl.ds(LANE, columns))

    loads = [
        pltpu.make_async_copy(state_ref, s0.at[(pl.ds(1, levels),) + inner], load_sem.at[0]),
        pltpu.make_async_copy(misfit_ref, misfit, load_sem.at[1]),
        pltpu.make_async_copy(east_ref, east, load_sem.at[2]),
        pltpu.make_async_copy(north_ref, north, load_sem.at[3]),
        pltpu.make_async_copy(land_ref, land, load_sem.at[4]),
    ]
    for load in loads:
        load.start()

    barrier = pltpu.get_barrier_semaphore()

    @pl.loop(1, tiles)
    def _(i):
        other = lax.rem(tile + i, tiles)
        pl.semaphore_signal(barrier, inc=1, device_id=(grp, other), device_id_type=MESH)

    @pl.when(grp > 0)
    def _():
        pl.semaphore_signal(barrier, inc=1, device_id=(grp - 1, tile), device_id_type=MESH)

    @pl.when(grp < grps - 1)
    def _():
        pl.semaphore_signal(barrier, inc=1, device_id=(grp + 1, tile), device_id_type=MESH)

    for buf in (s0, s1):
        for start in (0, columns + LANE):
            buf[1 : levels + 1, SUB : SUB + rows, start : start + LANE] = jnp.zeros(
                (levels, rows, LANE), jnp.float32
            )

        @pl.when(tile == 0)
        def _():
            buf[0, SUB : SUB + rows, :] = jnp.zeros((rows, columns + 2 * LANE), jnp.float32)

        @pl.when(tile == tiles - 1)
        def _():
            buf[levels + 1, SUB : SUB + rows, :] = jnp.zeros((rows, columns + 2 * LANE), jnp.float32)

        @pl.when(grp == 0)
        def _():
            buf[1 : levels + 1, 0:SUB, :] = jnp.zeros((levels, SUB, columns + 2 * LANE), jnp.float32)

        @pl.when(grp == grps - 1)
        def _():
            buf[1 : levels + 1, SUB + rows :, :] = jnp.zeros(
                (levels, SUB, columns + 2 * LANE), jnp.float32
            )

    beside = (grp > 0).astype(jnp.int32) + (grp < grps - 1).astype(jnp.int32)
    pl.semaphore_wait(barrier, tiles - 1 + beside)

    def level_copies(buf, step):
        top, bottom = state_ref.at[0], state_ref.at[levels - 1]
        if step:
            top, bottom = buf.at[(1,) + inner], buf.at[(levels,) + inner]
        return [
            (
                tile > 0,
                tile < tiles - 1,
                pltpu.make_async_remote_copy(
                    top,
                    buf.at[(levels + 1,) + inner],
                    level_send.at[step, 0],
                    level_recv.at[step, 0],
                    (grp, tile - 1),
                    MESH,
                ),
            ),
            (
                tile < tiles - 1,
                tile > 0,
                pltpu.make_async_remote_copy(
                    bottom,
                    buf.at[(0,) + inner],
                    level_send.at[step, 1],
                    level_recv.at[step, 1],
                    (grp, tile + 1),
                    MESH,
                ),
            ),
        ]

    def row_copies(buf, step, slot, first, count):
        span = pl.ds(first + 1, count)
        across = pl.ds(LANE, columns)
        top, bottom = state_ref.at[:, pl.ds(0, 1), :], state_ref.at[:, pl.ds(rows - 1, 1), :]
        if step:
            top = buf.at[span, pl.ds(SUB, 1), across]
            bottom = buf.at[span, pl.ds(SUB + rows - 1, 1), across]
        return [
            (
                grp > 0,
                grp < grps - 1,
                pltpu.make_async_remote_copy(
                    top,
                    buf.at[span, pl.ds(SUB + rows, 1), across],
                    row_send.at[slot, 0],
                    row_recv.at[slot, 0],
                    (grp - 1, tile),
                    MESH,
                ),
            ),
            (
                grp < grps - 1,
                grp > 0,
                pltpu.make_async_remote_copy(
                    bottom,
                    buf.at[span, pl.ds(SUB - 1, 1), across],
                    row_send.at[slot, 1],
                    row_recv.at[slot, 1],
                    (grp + 1, tile),
                    MESH,
                ),
            ),
        ]

    def start(copies):
        for sends, _, copy in copies:
            pl.when(sends)(copy.start)

    def arrive(copies):
        for _, receives, copy in copies:
            pl.when(receives)(copy.wait_recv)

    def leave(copies):
        for sends, _, copy in copies:
            pl.when(sends)(copy.wait_send)

    sub_index = lax.broadcasted_iota(jnp.int32, (SUB, WIDTH), 0)

    def advance(src, dst, pad, first, count, row_first, row_count):
        if count <= 0:
            return

        @pl.loop(0, count * row_count)
        def _(i):
            level = first + lax.div(i, row_count)
            row = pl.multiple_of((row_first + lax.rem(i, row_count)) * SUB, SUB)
            for at in range(0, columns, WIDTH):
                here = pl.ds(at, WIDTH)
                mid = pl.ds(at + LANE, WIDTH)
                wide = src[level + 1, pl.ds(row + SUB, SUB), pl.ds(at, WIDTH + 2 * LANE)]
                center = wide[:, LANE : LANE + WIDTH]
                e = pltpu.roll(wide, WIDTH + 2 * LANE - 1, 1)[:, LANE : LANE + WIDTH]
                w = pltpu.roll(wide, 1, 1)[:, LANE : LANE + WIDTH]
                up = src[level + 1, pl.ds(row, SUB), mid]
                down = src[level + 1, pl.ds(row + 2 * SUB, SUB), mid]
                n = pltpu.roll(jnp.where(sub_index == 0, down, center), SUB - 1, 0)
                s = pltpu.roll(jnp.where(sub_index == SUB - 1, up, center), 1, 0)
                a = src[level, pl.ds(row + SUB, SUB), mid]
                b = src[level + 2, pl.ds(row + SUB, SUB), mid]
                rr = pl.ds(row, SUB)
                flow = east[level, rr, here] * (e - w) + north[level, rr, here] * (n - s)
                value = (
                    (0.3 * center + misfit[level, rr, here])
                    + 0.5 * flow
                    + (0.1 * ((e + w) + (n + s)) + 0.15 * (a + b))
                )
                value = land[level, rr, here].astype(jnp.float32) * value
                if pad:
                    dst[level + 1, pl.ds(row + SUB, SUB), mid] = value
                else:
                    dst[level, rr, here] = value

    def forward(first, count, row_first, row_count):
        if count <= 0:
            return
        for r in range(row_first, row_first + row_count):
            span = pl.ds(r * SUB, SUB)
            target = pencil.at[pl.ds(tile * levels + first, count), span, :]

            @pl.loop(1, tiles)
            def _(i):
                other = lax.rem(tile + i, tiles)
                mine = pl.ds(pl.multiple_of(other * part, LANE), part)
                pltpu.make_async_remote_copy(
                    s2.at[pl.ds(first, count), span, mine],
                    target,
                    fwd_send,
                    fwd_recv.at[r],
                    (grp, other),
                    MESH,
                ).start()

            own = pl.ds(pl.multiple_of(tile * part, LANE), part)
            pltpu.make_async_copy(
                s2.at[pl.ds(first, count), span, own], target, fwd_recv.at[r]
            ).start()

    level0 = level_copies(s0, 0)
    row0 = row_copies(s0, 0, 0, 0, levels)
    start(row0)
    start(level0)
    for load in loads:
        load.wait()

    level1 = level_copies(s1, 1)
    row_mid = row_copies(s1, 1, 1, 1, levels - 2) if levels > 2 else []
    row_ends = row_copies(s1, 1, 2, 0, 1) + row_copies(s1, 1, 3, levels - 1, 1)
    early = levels - 2 * near
    middle = chunks - 2
    advance(s0, s1, True, 1, levels - 2, 1, middle)
    arrive(row0)
    advance(s0, s1, True, 1, levels - 2, 0, 1)
    for r in range(1, middle):
        advance(s1, s2, False, near, early, r, 1)
        forward(near, early, r, 1)
    advance(s0, s1, True, 1, levels - 2, chunks - 1, 1)
    start(row_mid)
    advance(s1, s2, False, near, early, middle, 1)
    forward(near, early, middle, 1)

    arrive(level0)
    advance(s0, s1, True, 0, 1, 0, chunks)
    advance(s0, s1, True, levels - 1, 1, 0, chunks)
    start(level1)
    start(row_ends)

    arrive(row_mid)
    for r in (0, chunks - 1):
        advance(s1, s2, False, near, early, r, 1)
        forward(near, early, r, 1)
    advance(s1, s2, False, 1, near - 1, 0, chunks)
    advance(s1, s2, False, levels - near, near - 1, 0, chunks)

    size = tiles * levels * SUB
    repeat = (
        lax.shift_right_logical(lax.broadcasted_iota(jnp.int32, (size, tiles * levels), 0), 3)
        == lax.broadcasted_iota(jnp.int32, (size, tiles * levels), 1)
    ).astype(jnp.float32)
    tall = jnp.dot(repeat, matrix_ref[...], precision=HIGHEST, preferred_element_type=jnp.float32)
    full = lax.dot_general(
        tall,
        repeat,
        (((1,), (1,)), ((), ())),
        precision=HIGHEST,
        preferred_element_type=jnp.float32,
    )
    same = (lax.broadcasted_iota(jnp.int32, (size, size), 0) & (SUB - 1)) == (
        lax.broadcasted_iota(jnp.int32, (size, size), 1) & (SUB - 1)
    )
    kron[...] = jnp.where(same, full, 0.0)

    arrive(level1)
    arrive(row_ends)
    order = list(range(1, chunks - 1)) + [0, chunks - 1]
    for r in order:
        advance(s1, s2, False, 0, 1, r, 1)
        advance(s1, s2, False, levels - 1, 1, r, 1)
        forward(0, near, r, 1)
        forward(levels - near, near, r, 1)

    for r in order:
        span = pl.ds(r * SUB, SUB)
        chunk = pencil.at[:, span, :]
        pltpu.make_async_copy(chunk, chunk, fwd_recv.at[r]).wait()
        result = jnp.dot(
            kron[...],
            pencil[:, r * SUB : (r + 1) * SUB, :].reshape(size, part),
            precision=HIGHEST,
            preferred_element_type=jnp.float32,
        )
        smooth[:, r * SUB : (r + 1) * SUB, :] = result.reshape(tiles * levels, SUB, part)
        home = out_ref.at[:, span, pl.ds(pl.multiple_of(tile * part, LANE), part)]

        @pl.loop(1, tiles)
        def _(i):
            other = lax.rem(tile + i, tiles)
            pltpu.make_async_remote_copy(
                smooth.at[pl.ds(other * levels, levels), span, :],
                home,
                ret_send,
                ret_recv,
                (grp, other),
                MESH,
            ).start()

        pltpu.make_async_copy(
            smooth.at[pl.ds(tile * levels, levels), span, :], home, ret_recv
        ).start()
        surface_ref[r * SUB : (r + 1) * SUB, :] = result[0:SUB]

    for copies in (level0, row0, level1, row_mid, row_ends):
        leave(copies)
    sent = s2.at[:, :, pl.ds(0, (tiles - 1) * part)]
    pltpu.make_async_copy(sent, sent, fwd_send).wait()
    returned = smooth.at[pl.ds(0, (tiles - 1) * levels)]
    pltpu.make_async_copy(returned, returned, ret_send).wait()
    pltpu.make_async_copy(out_ref, out_ref, ret_recv).wait()


def body(tiles, grps, *args):
    args, select = args[:5] + args[6:], args[5]
    levels, rows, columns = args[0].shape
    part = columns // tiles
    total = tiles * levels
    padded = (levels + 2, rows + 2 * SUB, columns + 2 * LANE)
    block = (levels, rows, columns)
    anywhere = pl.BlockSpec(memory_space=pl.ANY)
    vmem = pl.BlockSpec(memory_space=pltpu.VMEM)
    filtered, surface = pl.pallas_call(
        functools.partial(kernel, tiles, grps),
        out_shape=(
            jax.ShapeDtypeStruct(block, jnp.float32),
            jax.ShapeDtypeStruct((rows, part), jnp.float32),
        ),
        in_specs=[anywhere] * 5 + [vmem],
        out_specs=(anywhere, vmem),
        scratch_shapes=[
            pltpu.VMEM(padded, jnp.float32),
            pltpu.VMEM(padded, jnp.float32),
            pltpu.VMEM(block, jnp.float32),
            pltpu.VMEM(block, jnp.float32),
            pltpu.VMEM(block, jnp.float32),
            pltpu.VMEM(block, jnp.float32),
            pltpu.VMEM(block, jnp.int32),
            pltpu.VMEM((total, rows, part), jnp.float32),
            pltpu.VMEM((total, rows, part), jnp.float32),
            pltpu.VMEM((total * SUB, total * SUB), jnp.float32),
            pltpu.SemaphoreType.DMA((5,)),
            pltpu.SemaphoreType.DMA((2, 2)),
            pltpu.SemaphoreType.DMA((2, 2)),
            pltpu.SemaphoreType.DMA((4, 2)),
            pltpu.SemaphoreType.DMA((4, 2)),
            pltpu.SemaphoreType.DMA,
            pltpu.SemaphoreType.DMA((rows // SUB,)),
            pltpu.SemaphoreType.DMA,
            pltpu.SemaphoreType.DMA,
        ],
        compiler_params=pltpu.CompilerParams(
            collective_id=0, has_side_effects=True, vmem_limit_bytes=56 * 1024 * 1024
        ),
    )(*args)
    return filtered, select.astype(jnp.float32) * surface


def solution(mesh):
    split = P("tile", "grp", None)
    return jax.shard_map(
        functools.partial(body, mesh.shape["tile"], mesh.shape["grp"]),
        mesh=mesh,
        in_specs=(split,) * 5 + (P("grp", "tile"), P()),
        out_specs=(split, P("grp", "tile")),
        check_vma=False,
    )
```
